32 devices in a mesh: groups: 2 (over y), wide: 4 (over z), narrow: 4 (over x, core).
Axes of the slice: x: 2, y: 2, z: 4, core: 2. Of those that a mesh axis runs over, the one named last changes fastest.
Arguments:
- layer_input_hidden: bfloat16 [8192, 5120], P(('groups', 'wide'), 'narrow'), parts along dimension 0, may hold values from -6 to 6
- token_adapter_index: int32 [8192, 1], P(('groups', 'wide')), parts along dimension 0, may hold values from 0 to 15; in each aligned block of 1024 rows (0 to 1023, 1024 to 2047, ...) at most 128 rows name the same one
- frozen_value_weight: bfloat16 [5120, 1024], P('narrow'), may hold values from -0.078125 to 0.078125
- adapter_down_weight: bfloat16 [32, 5120, 64], P(('groups', 'wide'), 'narrow'), parts along dimension 0, may hold values from -0.078125 to 0.078125
- adapter_up_weight: bfloat16 [32, 64, 1024], P(('groups', 'wide'), None, 'narrow'), parts along dimension 0, may hold values from -0.1875 to 0.1875
- output_cotangent_rows: bfloat16 [8192, 1024], P(('groups', 'wide'), 'narrow'), parts along dimension 0, may hold values from -6 to 6
Outputs:
- projected: bfloat16 [8192, 1024], P(('groups', 'wide'), 'narrow'), parts along dimension 0
- input_grad: bfloat16 [8192, 5120], P(('groups', 'wide'), 'narrow'), parts along dimension 0
- grad_down: float32 [32, 5120, 64], P(('groups', 'wide'), 'narrow'), parts along dimension 0
- up_weight_gradient: float32 [32, 64, 1024], P(('groups', 'wide'), None, 'narrow'), parts along dimension 0
The draws below stay inside these ranges and needn't reach their ends.
There are 2 independent parts, one for each index of `groups`. The reference program is written for one: setup_inputs(seed, part) draws one part's arguments, and reference() takes and returns one part's arrays. A program takes and returns all parts, laid end to end along the dimension named above; an argument that names none is the same for every part. Nothing has to cross between parts.
Inputs may be any that keep to these rules, and one draw needn't show every extreme that they name: `token_adapter_index`: within each packed row of 1024 tokens no adapter serves more than 128 tokens, and some adapter serves exactly 128 tokens of some row; every adapter serves some token.
All inputs are finite; a program needn't handle non-finite values.
Results may differ from the reference program's by a relative error of at most 0.0037.
Values may be sent and summed in bfloat16 or wider, within the bound.
No kernel may reach another device: no remote copies, remote signals or barrier semaphores. Data moves between devices by JAX's collectives and lax.ppermute only.
A program may use at most 128 MiB of HBM per device.

```python
import math
import jax
import jax.numpy as jnp
import numpy as np
from jax import lax

MODEL_WIDTH = 5120
VALUE_FEATURES = 1024
ADAPTER_RANK = 64
TOKW = 1024
ADAPTER_COUNT = 16
CAP = 128
TOKENS = 4096
N_WIDE = 4


def block_scale(stream_key, extent, pieces, smallest, top_value):
    loudness = 1.0
    for position, shards_of in pieces:
        heights = jax.random.uniform(jax.random.fold_in(jax.random.fold_in(stream_key, 6), position), (shards_of,), jnp.float32, smallest / len(pieces), top_value / len(pieces))
        loudness = loudness * jnp.repeat(jnp.exp(heights), extent[position] // shards_of).reshape((-1,) + (1,) * (len(extent) - 1 - position))
    return loudness


def assign_block(stream_key, own, number, rows, number_of, top, reach, lean):
    ranking = jax.random.permutation(stream_key, number_of)
    heavy_load, common = portions_of(number_of, rows * top, reach, lean, True), portions_of(number_of, rows * top, reach, lean, False)
    places = jnp.arange(number_of)

    def named(sizes, rotation):
        used = int((sizes > 0).sum())
        fixed = max(1, used // 4)
        shifted = fixed + (places - fixed + rotation * (used - fixed)) % max(1, number_of - fixed)
        return jnp.zeros((number_of,), jnp.int32).at[ranking[jnp.where(places < fixed, places, shifted)]].set(jnp.asarray(sizes, jnp.int32))

    sizes = jnp.where(number % 4 == 0, named(heavy_load, number // 4), named(common, number - number // 4 - 1))
    mixed = jax.random.permutation(jax.random.fold_in(own, 3), number_of)
    giver, receiver = mixed[0:number_of // 2 * 2:2], mixed[1:number_of // 2 * 2:2]
    slack = jnp.minimum(sizes[giver] - 1, reach - sizes[receiver]) // 2
    slack = jnp.where((giver == ranking[0]) | (receiver == ranking[0]) | (sizes[receiver] == 0), 0, jnp.maximum(slack, 0))
    shifted = jax.random.randint(jax.random.fold_in(own, 4), (number_of // 2,), 0, 1 << 20) % (slack + 1)
    sizes = sizes.at[giver].add(-shifted).at[receiver].add(shifted)
    members = jnp.searchsorted(jnp.cumsum(sizes), jnp.arange(rows * top), side="right").astype(jnp.int32)
    grid = members.reshape(top, rows).T
    grid = grid[jax.random.permutation(jax.random.fold_in(own, 1), rows)]
    rotation = jax.random.randint(jax.random.fold_in(own, 2), (rows, 1), 0, top)
    return jnp.take_along_axis(grid, (jnp.arange(top)[None, :] + rotation) % top, axis=1)


def portions_of(number_of, total, limit, skew, full):
    loads = [(1 << 20) // math.isqrt(grade ** skew) + 1 for grade in range(1, number_of + 1)]
    largest = limit if full else min(limit, max(-(-total // number_of), total * loads[0] // sum(loads)))
    least = 1 if total - largest >= number_of - 1 else 0
    holding, rest = [largest] + [least] * (number_of - 1), total - largest - least * (number_of - 1)
    while rest > 0:
        free = [i for i in range(1, number_of) if holding[i] < largest] or [i for i in range(1, number_of) if holding[i] < limit]
        mass, left = sum([loads[i] for i in free]), rest
        for i in free:
            more = min(limit - holding[i], max(1, left * loads[i] // mass), rest)
            holding[i] = holding[i] + more
            rest = rest - more
    return np.array(holding)


def gaussian(key, extent, scale, reach, pieces=(), kind=jnp.bfloat16):
    values = jax.random.normal(key, extent, jnp.float32) * scale
    if len(pieces) > 0:
        values = block_scale(key, extent, pieces, -0.22, 0.18) * values
    return jnp.clip(values, min=-reach, max=reach).astype(kind)


def setup_inputs(seed: int = 0, part: int = 0) -> dict:
    seeds = jax.random.split(jax.random.key(seed), 7)
    part_splits = jax.random.split(jax.random.fold_in(seeds[6], part), 7)
    layer_input_hidden = gaussian(part_splits[0], (TOKENS, MODEL_WIDTH), 1.0, 6.0, ((0, 4), (1, 4)))
    token_adapter_index_keys = jax.random.split(jax.random.fold_in(part_splits[1], 1), TOKENS // TOKW)
    token_adapter_index_turns = jax.random.permutation(jax.random.fold_in(part_splits[1], 3), TOKENS // TOKW)
    token_adapter_index = jax.vmap(lambda own, number: assign_block(jax.random.fold_in(part_splits[1], 2), own, number, TOKW, ADAPTER_COUNT, 1, CAP, 2))(token_adapter_index_keys, token_adapter_index_turns).reshape((TOKENS, 1))
    frozen_value_weight = gaussian(seeds[2], (MODEL_WIDTH, VALUE_FEATURES), MODEL_WIDTH ** -0.5, 0.078125, ((0, 4),))
    adapter_down_weight = gaussian(part_splits[3], (ADAPTER_COUNT, MODEL_WIDTH, ADAPTER_RANK), MODEL_WIDTH ** -0.5, 0.078125, ((0, 4), (1, 4)))
    adapter_up_weight = gaussian(part_splits[4], (ADAPTER_COUNT, ADAPTER_RANK, VALUE_FEATURES), VALUE_FEATURES ** -0.5, 0.1875, ((0, 4), (2, 4)))
    output_cotangent_rows = gaussian(part_splits[5], (TOKENS, VALUE_FEATURES), 1.0, 6.0, ((0, 4), (1, 4)))
    return dict(layer_input_hidden=layer_input_hidden, token_adapter_index=token_adapter_index, frozen_value_weight=frozen_value_weight, adapter_down_weight=adapter_down_weight, adapter_up_weight=adapter_up_weight, output_cotangent_rows=output_cotangent_rows)


ADAPTER_SCALE = 2.0


def reference(layer_input_hidden, token_adapter_index, frozen_value_weight, adapter_down_weight, adapter_up_weight, output_cotangent_rows):
    total_slot_count = ADAPTER_COUNT * CAP
    down_weight_gathered = adapter_down_weight.astype(jnp.float32)
    up_weight_gathered = adapter_up_weight.astype(jnp.float32)
    row_feats = layer_input_hidden.reshape(N_WIDE, TOKW, MODEL_WIDTH)
    row_labels = token_adapter_index.reshape(N_WIDE, TOKW)
    row_cots = output_cotangent_rows.reshape(N_WIDE, TOKW, VALUE_FEATURES)

    def one_row(running, inputs):
        grad_down, up_weight_gradient = running
        feats_now, labels, cots_now = inputs
        onehot = (labels[:, None] == jnp.arange(ADAPTER_COUNT, dtype=jnp.int32)[None, :]).astype(jnp.int32)
        earlier = jnp.cumsum(onehot, axis=0) - onehot
        slot_ids = (labels * CAP + jnp.sum(earlier * onehot, axis=1)).astype(jnp.int32)
        features = jnp.zeros((total_slot_count, MODEL_WIDTH), jnp.float32).at[slot_ids].set(feats_now.astype(jnp.float32))
        features = features.reshape(ADAPTER_COUNT, CAP, MODEL_WIDTH)
        cotangent_token_rows = jnp.zeros((total_slot_count, VALUE_FEATURES), jnp.float32).at[slot_ids].set(cots_now.astype(jnp.float32))
        cotangent_token_rows = cotangent_token_rows.reshape(ADAPTER_COUNT, CAP, VALUE_FEATURES)
        rank_space_state = lax.optimization_barrier(jnp.einsum("acd,adr->acr", features, down_weight_gathered).astype(jnp.bfloat16)).astype(jnp.float32)
        backward_rank_rows = lax.optimization_barrier((ADAPTER_SCALE * jnp.einsum("dzh,djh->dzj", cotangent_token_rows, up_weight_gathered)).astype(jnp.bfloat16)).astype(jnp.float32)
        adapter_output_delta = (ADAPTER_SCALE * jnp.einsum("zht,ztm->zhm", rank_space_state, up_weight_gathered)).astype(jnp.bfloat16).reshape(total_slot_count, VALUE_FEATURES)
        input_term = jnp.einsum("acr,adr->acd", backward_rank_rows, down_weight_gathered).astype(jnp.bfloat16).reshape(total_slot_count, MODEL_WIDTH)
        up_weight_gradient = up_weight_gradient + ADAPTER_SCALE * jnp.einsum("ngd,nge->nde", rank_space_state, cotangent_token_rows)
        grad_down = grad_down + jnp.einsum("acd,acr->adr", features, backward_rank_rows)
        base_out = jnp.dot(feats_now, frozen_value_weight, preferred_element_type=jnp.float32)
        projected = (base_out + adapter_output_delta[slot_ids].astype(jnp.float32)).astype(jnp.bfloat16)
        base_back = lax.dot_general(cots_now, frozen_value_weight, (((1,), (1,)), ((), ())), preferred_element_type=jnp.float32)
        input_grad = (base_back + input_term[slot_ids].astype(jnp.float32)).astype(jnp.bfloat16)
        return (grad_down, up_weight_gradient), (projected, input_grad)

    start_grads = (jnp.zeros((ADAPTER_COUNT, MODEL_WIDTH, ADAPTER_RANK), jnp.float32), jnp.zeros((ADAPTER_COUNT, ADAPTER_RANK, VALUE_FEATURES), jnp.float32))
    final_grads, outputs = lax.scan(one_row, start_grads, (row_feats, row_labels, row_cots))
    projected = outputs[0].reshape(TOKENS, VALUE_FEATURES)
    input_grad = outputs[1].reshape(TOKENS, MODEL_WIDTH)
    return (projected, input_grad, final_grads[0], final_grads[1])
```

```python
import jax
import jax.numpy as jnp
from jax import lax
from jax.sharding import PartitionSpec as P

ADAPTER_SCALE = 2.0
F32 = jnp.float32
BF16 = jnp.bfloat16


def mask_of(labels, block, per_owner):
    names = block * per_owner + jnp.arange(per_owner, dtype=jnp.int32)
    return labels[None, :] == names[:, None]


def pick(products, labels, block, per_owner):
    rank, tokens = products.shape[0] // per_owner, products.shape[1]
    mask = mask_of(labels, block, per_owner)
    return jnp.sum(
        jnp.where(mask[:, None, :], products.reshape(per_owner, rank, tokens), 0.0), axis=0
    )


def spread(values, labels, block, per_owner):
    rank, tokens = values.shape
    mask = mask_of(labels, block, per_owner)
    wide = jnp.where(mask[:, None, :], values[None], jnp.zeros((), values.dtype))
    return wide.reshape(per_owner * rank, tokens)


def matmul(left, right):
    return jnp.dot(left, right, preferred_element_type=F32)


def matmul_nt(left, right):
    return lax.dot_general(left, right, (((1,), (1,)), ((), ())), preferred_element_type=F32)


def matmul_tn(left, right):
    return lax.dot_general(left, right, (((0,), (0,)), ((), ())), preferred_element_type=F32)


def gather_cyclic(block):
    owners = lax.axis_size("wide")
    return [block] + [
        lax.ppermute(block, "wide", [((k + m) % owners, k) for k in range(owners)])
        for m in range(1, owners)
    ]


def gather_line(block):
    owners, me = lax.axis_size("wide"), lax.axis_index("wide")
    from_left = from_right = block
    pieces = [(block, me)]
    for k in range(1, owners):
        from_left = lax.ppermute(
            from_left, "wide", [(d, d + 1) for d in range(k - 1, owners - 1)]
        )
        from_right = lax.ppermute(
            from_right, "wide", [(d, d - 1) for d in range(1, owners - k + 1)]
        )
        if 2 * k < owners:
            pieces += [(from_left, me - k), (from_right, me + k)]
        else:
            right_valid = me + k < owners
            pieces.append(
                (
                    jnp.where(right_valid, from_right, from_left),
                    jnp.where(right_valid, me + k, me - k),
                )
            )
    return pieces


def scatter_line(terms):
    owners = lax.axis_size("wide")
    to_right = to_left = 0.0
    for step in range(1, owners):
        to_right = lax.ppermute(
            (terms[owners - step] + to_right).astype(BF16),
            "wide",
            [(d, d + 1) for d in range(step) if d + 1 < owners],
        ).astype(F32)
        to_left = lax.ppermute(
            (terms[step] + to_left).astype(BF16),
            "wide",
            [(d, d - 1) for d in range(owners - step, owners) if d > 0],
        ).astype(F32)
    return terms[0] + to_right + to_left


def sum_narrow(values):
    size = lax.axis_size("narrow")
    step = 1
    while step < size:
        values = values + lax.ppermute(values, "narrow", [(d, d ^ step) for d in range(size)])
        step *= 2
    return values


def body(x, token_adapter_index, weight, down, up, cot):
    owners, me = lax.axis_size("wide"), lax.axis_index("wide")
    per_owner, width_part, rank = down.shape
    value_part = up.shape[2]
    rows = per_owner * rank
    labels = token_adapter_index[:, 0]
    down_own = jnp.swapaxes(down, 1, 2).reshape(rows, width_part)
    up_own = up.reshape(rows, value_part)
    blocks = [(me + m) % owners for m in range(owners)]

    up_all = gather_cyclic(up_own)
    down_all = gather_line(down_own)

    back = sum(
        pick(matmul_nt(u, cot), labels, b, per_owner) for u, b in zip(up_all, blocks)
    )
    back = (ADAPTER_SCALE * sum_narrow(back)).astype(BF16)
    down_terms = [matmul(spread(back, labels, b, per_owner), x) for b in blocks]
    grad_down = scatter_line(down_terms)

    partial_out = matmul(x, weight)
    base_out = lax.psum_scatter(partial_out, "narrow", scatter_dimension=1, tiled=True)
    cot_all = lax.all_gather(cot, "narrow", axis=1, tiled=True)
    base_back = matmul_nt(cot_all, weight)

    low = sum(pick(matmul_nt(d, x), labels, b, per_owner) for d, b in down_all)
    low = sum_narrow(low).astype(BF16)
    low_wide = [spread(low, labels, b, per_owner) for b in blocks]
    up_terms = [ADAPTER_SCALE * matmul(wide, cot) for wide in low_wide]
    grad_up = scatter_line(up_terms)

    update = ADAPTER_SCALE * matmul_tn(
        jnp.concatenate(low_wide, axis=0), jnp.concatenate(up_all, axis=0)
    )
    projected = (base_out + update.astype(BF16).astype(F32)).astype(BF16)
    input_term = matmul_tn(
        jnp.concatenate([spread(back, labels, b, per_owner) for _, b in down_all], axis=0),
        jnp.concatenate([d for d, _ in down_all], axis=0),
    )
    input_grad = (base_back + input_term.astype(BF16).astype(F32)).astype(BF16)

    return (
        projected,
        input_grad,
        jnp.swapaxes(grad_down.reshape(per_owner, rank, width_part), 1, 2),
        grad_up.reshape(per_owner, rank, value_part),
    )


def solution(mesh):
    in_specs = (
        P(("groups", "wide"), "narrow"),
        P(("groups", "wide"), None),
        P("narrow", None),
        P(("groups", "wide"), "narrow", None),
        P(("groups", "wide"), None, "narrow"),
        P(("groups", "wide"), "narrow"),
    )
    out_specs = (
        P(("groups", "wide"), "narrow"),
        P(("groups", "wide"), "narrow"),
        P(("groups", "wide"), "narrow", None),
        P(("groups", "wide"), None, "narrow"),
    )
    return jax.shard_map(body, mesh=mesh, in_specs=in_specs, out_specs=out_specs, check_vma=False)
```

```python
import functools

import jax
import jax.numpy as jnp
from jax import lax
from jax.experimental import pallas as pl
from jax.experimental.pallas import tpu as pltpu
from jax.sharding import PartitionSpec as P

ADAPTER_SCALE = 2.0
F32 = jnp.float32
BF16 = jnp.bfloat16
VMEM_BYTES = 16 * 1024 * 1024
FILLER_FLOPS = 8 * 10**9
BACK_FLOPS = 4 * 10**9


def dot_nn(left, right):
    return jnp.dot(left, right, preferred_element_type=F32)


def dot_nt(left, right):
    return lax.dot_general(left, right, (((1,), (1,)), ((), ())), preferred_element_type=F32)


def dot_tn(left, right):
    return lax.dot_general(left, right, (((0,), (0,)), ((), ())), preferred_element_type=F32)


def tie(*values):
    return lax.optimization_barrier(values)


def local_kernel(name, kernel, outs, *operands, late=(), flops=0):
    late = [entry if isinstance(entry, tuple) else (entry,) for entry in late]
    sources = [array for entry in late for array in entry[:2]]
    slots = [jax.ShapeDtypeStruct(entry[0].shape, entry[0].dtype) for entry in late]

    def fetching(*refs):
        ins, refs = refs[: len(sources)], refs[len(sources) :]
        direct, refs = refs[: len(operands)], refs[len(operands) :]
        results, refs = refs[: len(outs)], refs[len(outs) :]
        fetched, semaphores = refs[: len(late)], refs[-1]
        ins, waits = iter(ins), []
        for i, entry in enumerate(late):
            copies = [
                pltpu.make_async_copy(next(ins), fetched[i], semaphores.at[i]) for _ in entry[:2]
            ]
            if len(copies) == 1:
                copies[0].start()
            else:
                first = entry[2]()
                pl.when(first)(copies[0].start)
                pl.when(jnp.logical_not(first))(copies[1].start)
            waits.append(copies[0])
        for copy in waits:
            copy.wait()
        kernel(*fetched, *direct, *results)

    scratch = [pltpu.VMEM(slot.shape, slot.dtype) for slot in slots]
    return pl.pallas_call(
        fetching if late else kernel,
        name=name,
        out_shape=[jax.ShapeDtypeStruct(s, t) for s, t in outs],
        in_specs=[pl.BlockSpec(memory_space=pl.ANY)] * len(sources)
        + [pl.BlockSpec(memory_space=pltpu.VMEM)] * len(operands),
        out_specs=[pl.BlockSpec(memory_space=pltpu.VMEM)] * len(outs),
        scratch_shapes=scratch + ([pltpu.SemaphoreType.DMA((len(late),))] if late else []),
        compiler_params=pltpu.CompilerParams(vmem_limit_bytes=VMEM_BYTES),
        cost_estimate=pl.CostEstimate(flops=flops, bytes_accessed=0, transcendentals=0),
    )(*sources, *operands)


def tile_of(extent):
    return 256 if extent % 256 == 0 else 128


def spread_tile(values, places, offset, per_owner):
    return jnp.concatenate(
        [
            jnp.where(places == offset * per_owner + a, values, jnp.zeros((), values.dtype))
            for a in range(per_owner)
        ],
        axis=0,
    )


def pick_kernel(offsets, per_owner, has_start, halved, *refs):
    count = len(offsets)
    pieces, (places, rhs), rest = refs[:count], refs[count : count + 2], refs[count + 2 :]
    start, outs = (rest[0], rest[1:]) if has_start else (None, rest)
    tokens = rhs.shape[0]
    tile = tile_of(tokens)
    rank = pieces[0].shape[0] // per_owner
    core = lax.axis_index("narrow") % 2
    for i in range(tokens // tile):
        at = pl.ds(i * tile, tile)
        here, right = places[:, at], rhs[at, :]
        total = jnp.zeros((rank, tile), F32) if start is None else start[:, at]
        for piece, offset in zip(pieces, offsets):
            products = dot_nt(piece[...], right)
            for a in range(per_owner):
                total += jnp.where(
                    here == offset() * per_owner + a, products[a * rank : (a + 1) * rank], 0.0
                )
        if halved:
            low, high = total[: rank // 2], total[rank // 2 :]
            outs[0][:, at] = jnp.where(core == 0, low, high)
            outs[1][:, at] = jnp.where(core == 0, high, low)
        else:
            outs[0][:, at] = total


def pick(name, pieces, places, rhs, per_owner, start=None, halved=False, flops=0):
    rows = (pieces[0][0][0] if isinstance(pieces[0][0], tuple) else pieces[0][0]).shape[0]
    rank, tokens = rows // per_owner, rhs.shape[0]
    kernel = functools.partial(
        pick_kernel, [o for _, o in pieces], per_owner, start is not None, halved
    )
    more = [] if start is None else [start]
    outs = [((rank // 2, tokens), F32)] * 2 if halved else [((rank, tokens), F32)]
    outs = local_kernel(
        name, kernel, outs, places, rhs, *more, late=[p for p, _ in pieces], flops=flops
    )
    return outs if halved else outs[0]


def whole(mine, other):
    first = lax.axis_index("narrow") % 2 == 0
    return jnp.concatenate(
        [jnp.where(first, mine[...], other[...]), jnp.where(first, other[...], mine[...])], axis=0
    )


def terms_kernel(offsets, per_owner, scale, other, mine, places, rhs, *outs):
    tile = tile_of(rhs.shape[1])
    values = whole(mine, other)
    for offset, out in zip(offsets, outs):
        wide = spread_tile(values, places[...], offset(), per_owner)

        def step(i, carry, wide=wide, out=out):
            at = pl.ds(pl.multiple_of(i * tile, tile), tile)
            out[:, at] = (scale * dot_nn(wide, rhs[:, at])).astype(out.dtype)
            return carry

        lax.fori_loop(0, rhs.shape[1] // tile, step, 0, unroll=True)


def outer_terms(name, values, places, rhs, offsets, types, per_owner, scale):
    mine, other = values
    shape = (2 * mine.shape[0] * per_owner, rhs.shape[1])
    kernel = functools.partial(terms_kernel, offsets, per_owner, scale)
    return local_kernel(
        name, kernel, [(shape, t) for t in types], mine, places, rhs, late=[other]
    )


def send_kernel(sides, owners, *refs):
    me = lax.axis_index("wide")
    got, terms, outs = refs[:2], refs[2:4], refs[4:]
    tile = 64
    for (step, even_to_right, moving, summing), came, term, out in zip(sides, got, terms, outs):
        to_right = (me % 2 == 0) == even_to_right
        passes_on = jnp.where(to_right, me >= step, me + step < owners)
        for i in range(out.shape[0] // tile):
            at = pl.ds(i * tile, tile)
            value = came[at, :]
            if summing:
                total = (term[at, :] + value.astype(F32)).astype(BF16)
                value = jnp.where(passes_on, value, total) if moving else total
            out[at, :] = value


def base_kernel(x, weight, *outs):
    part, width = lax.axis_index("narrow"), outs[0].shape[1]
    for s, out in enumerate(outs):
        columns = pl.ds(pl.multiple_of((part ^ s) * width, width), width)

        def step(i, carry, out=out, columns=columns):
            at = pl.ds(pl.multiple_of(i * 256, 256), 256)
            out[at, :] = dot_nn(x[at, :], weight[:, columns])
            return carry

        lax.fori_loop(0, x.shape[0] // 256, step, 0, unroll=True)


def input_grad_kernel(offsets, per_owner, parts, *refs):
    count = len(offsets)
    pieces, cots = refs[:count], refs[count : count + parts]
    weight, mine, other, places, out = refs[count + parts :]
    part, width = lax.axis_index("narrow"), cots[0].shape[1]
    tile = 256
    values = whole(mine, other)

    for i in range(out.shape[0] // tile):
        at = pl.ds(i * tile, tile)
        term = jnp.zeros((tile, out.shape[1]), F32)
        for piece, offset in zip(pieces, offsets):
            term += dot_tn(
                spread_tile(
                    values[:, i * tile : (i + 1) * tile], places[:, at], offset(), per_owner
                ),
                piece[...],
            )
        total = term.astype(BF16).astype(F32)
        for s, cot in enumerate(cots):
            columns = pl.ds(pl.multiple_of((part ^ s) * width, width), width)
            total += dot_nt(cot[at, :], weight[:, columns])
        out[at, :] = total.astype(out.dtype)


def projected_kernel(offsets, per_owner, *refs):
    ups = refs[: len(offsets)]
    base, mine, other, places, out = refs[len(offsets) :]
    values = whole(mine, other)
    tile = 256
    for i in range(out.shape[0] // tile):
        at = pl.ds(i * tile, tile)
        update = jnp.zeros((tile, out.shape[1]), F32)
        for offset, up in zip(offsets, ups):
            here = values[:, i * tile : (i + 1) * tile]
            update += dot_tn(spread_tile(here, places[:, at], offset(), per_owner), up[...])
        update = (ADAPTER_SCALE * update).astype(BF16).astype(F32)
        out[at, :] = (base[at, :] + update).astype(out.dtype)


def pair_lists(right_senders, left_senders):
    return [
        [(d, d + 1) for d in right_senders if d % 2 == odd]
        + [(d, d - 1) for d in left_senders if d % 2 != odd]
        for odd in (0, 1)
    ]


def shift(value, pairs):
    return lax.ppermute(value, "wide", pairs) if pairs else None


def swap_narrow(value, bit):
    size = lax.axis_size("narrow")
    return lax.ppermute(value, "narrow", [(d, d ^ bit) for d in range(size)])


def narrow_bits():
    size, bits = lax.axis_size("narrow"), []
    while 1 << len(bits) < size:
        bits.append(1 << len(bits))
    return bits


def sum_narrow(mine, other, scale, held=()):
    bits = narrow_bits()
    mine = mine + swap_narrow(other, bits[0])
    mine, *held = tie(mine, *held)
    for bit in bits[1:]:
        mine = mine + swap_narrow(mine, bit)
    mine = (scale * mine).astype(BF16)
    return (mine, swap_narrow(mine, bits[0])), held


def body(x, token_adapter_index, weight, down, up, cot):
    owners, me = lax.axis_size("wide"), lax.axis_index("wide")
    parts = lax.axis_size("narrow")
    per_owner, width_part, rank = down.shape
    value_part = up.shape[2]
    rows = per_owner * rank
    tokens = x.shape[0]
    adapters = owners * per_owner
    last = owners - 1
    down_own = jnp.swapaxes(down, 1, 2).reshape(rows, width_part)
    up_own = up.reshape(rows, value_part)
    places = token_adapter_index[:, 0][None, :] - me * per_owner
    places = jnp.where(places < 0, places + adapters, places)

    def fixed(offset):
        return lambda: offset

    def by_side(at_even, at_odd):
        return lambda: jnp.where(lax.axis_index("wide") % 2 == 0, at_even, at_odd)

    def arriving(step, even_from_right):
        def offset():
            me = lax.axis_index("wide")
            from_right = (me % 2 == 0) == even_from_right
            right = jnp.where(me + step < owners, step, -owners)
            left = jnp.where(me >= step, owners - step, -owners)
            return jnp.where(from_right, right, left)

        return offset

    def from_a(step):
        def valid():
            me = lax.axis_index("wide")
            return jnp.where(me % 2 == 0, me + step < owners, me >= step)

        return valid

    def gather_pairs(step):
        return pair_lists(range(step - 1, last), range(1, owners - step + 1))

    def reduce_pairs(step):
        return pair_lists(range(min(step, last)), range(max(owners - step, 1), owners))

    right, left = range(last), range(1, owners)
    pairs_a, pairs_b = pair_lists(right, left)

    def across(bits):
        def offset():
            me = lax.axis_index("wide")
            return (me ^ bits) - me + jnp.where((me ^ bits) < me, owners, 0)

        return offset

    up_all = [(up_own, fixed(0))] + [
        (shift(up_own, [(d ^ bits, d) for d in range(owners)]), across(bits))
        for bits in range(1, owners)
    ]
    got_b = shift(down_own, pairs_b)
    got_a = shift(down_own, pairs_a)
    near, x_late = tie(up_all[1][0], x)
    up_all[1] = (near, up_all[1][1])
    low = pick("pick_own", [(down_own, fixed(0))], places, x_late, per_owner)

    cot_here, low = tie(cot, low)
    back = pick("pick_back", up_all, places, cot_here, per_owner, halved=True, flops=BACK_FLOPS)
    back, (got_a, got_b) = sum_narrow(*back, ADAPTER_SCALE, (got_a, got_b))

    (term_first,) = outer_terms(
        "terms_first", back, places, x, [by_side(owners - 1, 1)], [F32], per_owner, 1.0
    )
    offsets = [fixed(0)] + [by_side(owners - s, s) for s in range(2, owners)]
    terms = outer_terms("terms_rest", back, places, x, offsets, [F32] * len(offsets), per_owner, 1.0)
    terms = [terms[0], term_first, *terms[1:]]

    base = local_kernel("base", base_kernel, [((tokens, value_part), F32)] * parts, x_late, weight)
    sums = dict(enumerate(base))
    cots = {0: cot}
    near_bit, *far_bits = narrow_bits()

    def sum_base(bit):
        for s in [s for s in sums if s & bit]:
            value = sums.pop(s)
            value = value if bit == near_bit else value.astype(BF16)
            sums[s ^ bit] = sums[s ^ bit] + swap_narrow(value, bit).astype(F32)

    def gather_cots(bit):
        for s in list(cots):
            cots[s | bit] = swap_narrow(cots[s], bit)

    pieces = {}
    for step in range(1, owners):
        gathers, reduces = gather_pairs(step + 1), reduce_pairs(step)
        sides = [
            (step, True, bool(gathers[0]), bool(reduces[0])),
            (step, False, bool(gathers[1]), bool(reduces[1])),
        ]
        if sides[0][3] and sides[1][3]:
            send_a, send_b = local_kernel(
                f"send_{step}",
                functools.partial(send_kernel, sides, owners),
                [(down_own.shape, BF16)] * 2,
                terms[step],
                terms[owners - step],
                late=[got_b, got_a],
            )
        else:
            send_a = got_b
            if sides[0][3]:
                (send_a,) = local_kernel(
                    f"send_{step}",
                    lambda came, term, out, sides=sides: send_kernel(
                        sides[:1], owners, came, came, term, term, out
                    ),
                    [(down_own.shape, BF16)],
                    terms[step],
                    late=[got_b],
                )
            send_b = got_a
        send_a, send_b, got_a, got_b = tie(send_a, send_b, got_a, got_b)
        if step == 1:
            sum_base(near_bit)
            for bit in far_bits:
                gather_cots(bit)
        elif step == 2:
            held = [(cots, s) for s in cots] + [(sums, s) for s in sums]
            send_a, send_b, low, *values = tie(send_a, send_b, low, *[d[s] for d, s in held])
            for (d, s), value in zip(held, values):
                d[s] = value
            for bit in far_bits:
                sum_base(bit)
            gather_cots(near_bit)
        elif step == last:
            held = [(cots, s) for s in cots] + [(sums, s) for s in sums]
            send_a, send_b, low, *values = tie(send_a, send_b, low, *[d[s] for d, s in held])
            for (d, s), value in zip(held, values):
                d[s] = value
        live_a, live_b = gather_pairs(step)
        if live_a:
            pieces["a", step] = got_a
        if live_b:
            pieces["b", step] = got_b
        if step < last:
            arrived = [
                (pieces[side, step], arriving(step, side == "a"))
                for side in "ab"
                if (side, step) in pieces
            ]
        if 2 * step == owners:
            arrived = [((got_a, got_b, from_a(step)), by_side(step, owners - step))]
        elif step == last:
            arrived = [(got_a, arriving(step, True))]
        got_b = shift(send_b, pairs_b)
        got_a = shift(send_a, pairs_a)
        low = pick(f"pick_{step}", arrived, places, x, per_owner, low, step == last)
    places_late, got_a, got_b = tie(places, got_a, got_b)
    grad_down = terms[0] + got_a.astype(F32) + got_b.astype(F32)

    low, _ = sum_narrow(*low, 1.0)
    grad_up, *up_terms = outer_terms(
        "up_terms",
        low,
        places,
        cot,
        [fixed(m) for m in range(owners)],
        [F32] + [BF16] * last,
        per_owner,
        ADAPTER_SCALE,
    )
    got_up = [
        shift(term, [(d, (d + m) % owners) for d in range(owners)])
        for m, term in enumerate(up_terms, 1)
    ]

    projected = local_kernel(
        "projected",
        functools.partial(projected_kernel, [o for _, o in up_all], per_owner),
        [((tokens, value_part), BF16)],
        sums[0],
        *low,
        places_late,
        late=[u for u, _ in up_all],
    )[0]
    slots = [(down_own, fixed(0))]
    for step in range(1, owners):
        a, b = pieces.get(("a", step)), pieces.get(("b", owners - step))
        slots.append(((a, b, from_a(step)) if b is not None else a, by_side(step, owners - step)))
    input_grad = local_kernel(
        "input_grad",
        functools.partial(input_grad_kernel, [o for _, o in slots], per_owner, parts),
        [((tokens, width_part), BF16)],
        *[cots[s] for s in range(parts)],
        weight,
        *back,
        places_late,
        late=[d for d, _ in slots],
        flops=FILLER_FLOPS,
    )[0]

    input_grad, projected, *got_up = tie(input_grad, projected, *got_up)
    for got in got_up:
        grad_up += got.astype(F32)
    return (
        projected,
        input_grad,
        jnp.swapaxes(grad_down.reshape(per_owner, rank, width_part), 1, 2),
        grad_up.reshape(per_owner, rank, value_part),
    )


def solution(mesh):
    in_specs = (
        P(("groups", "wide"), "narrow"),
        P(("groups", "wide"), None),
        P("narrow", None),
        P(("groups", "wide"), "narrow", None),
        P(("groups", "wide"), None, "narrow"),
        P(("groups", "wide"), "narrow"),
    )
    out_specs = (
        P(("groups", "wide"), "narrow"),
        P(("groups", "wide"), "narrow"),
        P(("groups", "wide"), "narrow", None),
        P(("groups", "wide"), None, "narrow"),
    )
    return jax.shard_map(body, mesh=mesh, in_specs=in_specs, out_specs=out_specs, check_vma=False)
```

```python
import functools

import jax
import jax.numpy as jnp
from jax import lax
from jax.experimental import pallas as pl
from jax.experimental.pallas import tpu as pltpu
from jax.sharding import PartitionSpec as P

ADAPTER_SCALE = 2.0
F32 = jnp.float32
BF16 = jnp.bfloat16
VMEM_BYTES = 16 * 1024 * 1024
FILLER_FLOPS = 8 * 10**9
BACK_FLOPS = 4 * 10**9
PICK_FLOPS = 4 * 10**9


def dot_nn(left, right):
    return jnp.dot(left, right, preferred_element_type=F32)


def dot_nt(left, right):
    return lax.dot_general(left, right, (((1,), (1,)), ((), ())), preferred_element_type=F32)


def dot_tn(left, right):
    return lax.dot_general(left, right, (((0,), (0,)), ((), ())), preferred_element_type=F32)


def tie(*values):
    return lax.optimization_barrier(values)


def local_kernel(name, kernel, outs, *operands, late=(), flops=0, stacked=False, scratch=()):
    late = [entry if isinstance(entry, tuple) else (entry,) for entry in late]
    sources = [array for entry in late for array in entry[:2]]
    slots = [jax.ShapeDtypeStruct(entry[0].shape, entry[0].dtype) for entry in late]

    def fetching(*refs):
        ins, refs = refs[: len(sources)], refs[len(sources) :]
        direct, refs = refs[: len(operands)], refs[len(operands) :]
        results, refs = refs[: len(outs)], refs[len(outs) :]
        extra, refs = refs[: len(scratch)], refs[len(scratch) :]
        semaphores = refs[-1]
        fetched = refs[:-1]
        if stacked:
            rows = slots[0].shape[0]
            fetched = [fetched[0].at[pl.ds(i * rows, rows)] for i in range(len(late))]
        ins, waits = iter(ins), []
        for i, entry in enumerate(late):
            copies = [
                pltpu.make_async_copy(next(ins), fetched[i], semaphores.at[i]) for _ in entry[:2]
            ]
            if len(copies) == 1:
                copies[0].start()
            else:
                first = entry[2]()
                pl.when(first)(copies[0].start)
                pl.when(jnp.logical_not(first))(copies[1].start)
            waits.append(copies[0])
        for copy in waits:
            copy.wait()
        kernel(*(refs[:1] if stacked else fetched), *direct, *results, *extra)

    buffers = [pltpu.VMEM(slot.shape, slot.dtype) for slot in slots]
    if stacked:
        rows, columns = slots[0].shape
        buffers = [pltpu.VMEM((len(slots) * rows, columns), slots[0].dtype)]
    return pl.pallas_call(
        fetching if late else kernel,
        name=name,
        out_shape=[jax.ShapeDtypeStruct(s, t) for s, t in outs],
        in_specs=[pl.BlockSpec(memory_space=pl.ANY)] * len(sources)
        + [pl.BlockSpec(memory_space=pltpu.VMEM)] * len(operands),
        out_specs=[pl.BlockSpec(memory_space=pltpu.VMEM)] * len(outs),
        scratch_shapes=[
            *scratch,
            *buffers,
            *([pltpu.SemaphoreType.DMA((len(late),))] if late else []),
        ],
        compiler_params=pltpu.CompilerParams(vmem_limit_bytes=VMEM_BYTES),
        cost_estimate=pl.CostEstimate(flops=flops, bytes_accessed=0, transcendentals=0),
    )(*sources, *operands)


def tile_of(extent):
    return 256 if extent % 256 == 0 else 128


def spread_tile(values, places, offset, per_owner):
    return jnp.concatenate(
        [
            jnp.where(places == offset * per_owner + a, values, jnp.zeros((), values.dtype))
            for a in range(per_owner)
        ],
        axis=0,
    )


def pick_kernel(offsets, per_owner, has_start, halved, *refs):
    count = len(offsets)
    pieces, (places, rhs), rest = refs[:count], refs[count : count + 2], refs[count + 2 :]
    start, outs = (rest[0], rest[1:]) if has_start else (None, rest)
    tokens = rhs.shape[0]
    tile = tile_of(tokens)
    rank = pieces[0].shape[0] // per_owner
    core = lax.axis_index("narrow") % 2
    for i in range(tokens // tile):
        at = pl.ds(i * tile, tile)
        here, right = places[:, at], rhs[at, :]
        total = jnp.zeros((rank, tile), F32) if start is None else start[:, at]
        for piece, offset in zip(pieces, offsets):
            products = dot_nt(piece[...], right)
            for a in range(per_owner):
                total += jnp.where(
                    here == offset() * per_owner + a, products[a * rank : (a + 1) * rank], 0.0
                )
        if halved:
            low, high = total[: rank // 2], total[rank // 2 :]
            outs[0][:, at] = jnp.where(core == 0, low, high)
            outs[1][:, at] = jnp.where(core == 0, high, low)
        else:
            outs[0][:, at] = total


def pick(name, pieces, places, rhs, per_owner, start=None, halved=False, flops=0):
    rows = (pieces[0][0][0] if isinstance(pieces[0][0], tuple) else pieces[0][0]).shape[0]
    rank, tokens = rows // per_owner, rhs.shape[0]
    kernel = functools.partial(
        pick_kernel, [o for _, o in pieces], per_owner, start is not None, halved
    )
    more = [] if start is None else [start]
    outs = [((rank // 2, tokens), F32)] * 2 if halved else [((rank, tokens), F32)]
    outs = local_kernel(
        name, kernel, outs, places, rhs, *more, late=[p for p, _ in pieces], flops=flops
    )
    return outs if halved else outs[0]


def whole(mine, other):
    first = lax.axis_index("narrow") % 2 == 0
    return jnp.concatenate(
        [jnp.where(first, mine[...], other[...]), jnp.where(first, other[...], mine[...])], axis=0
    )


def terms_kernel(offsets, per_owner, scale, other, mine, places, rhs, *outs):
    tile = tile_of(rhs.shape[1])
    values = whole(mine, other)
    for offset, out in zip(offsets, outs):
        wide = spread_tile(values, places[...], offset(), per_owner)

        def step(i, carry, wide=wide, out=out):
            at = pl.ds(pl.multiple_of(i * tile, tile), tile)
            out[:, at] = (scale * dot_nn(wide, rhs[:, at])).astype(out.dtype)
            return carry

        lax.fori_loop(0, rhs.shape[1] // tile, step, 0, unroll=True)


def outer_terms(name, values, places, rhs, offsets, types, per_owner, scale):
    mine, other = values
    shape = (2 * mine.shape[0] * per_owner, rhs.shape[1])
    kernel = functools.partial(terms_kernel, offsets, per_owner, scale)
    return local_kernel(
        name, kernel, [(shape, t) for t in types], mine, places, rhs, late=[other]
    )


def send_kernel(sides, owners, *refs):
    me = lax.axis_index("wide")
    got, terms, outs = refs[:2], refs[2:4], refs[4:]
    tile = 64
    for (step, even_to_right, moving, summing), came, term, out in zip(sides, got, terms, outs):
        to_right = (me % 2 == 0) == even_to_right
        passes_on = jnp.where(to_right, me >= step, me + step < owners)
        for i in range(out.shape[0] // tile):
            at = pl.ds(i * tile, tile)
            value = came[at, :]
            if summing:
                total = (term[at, :] + value.astype(F32)).astype(BF16)
                value = jnp.where(passes_on, value, total) if moving else total
            out[at, :] = value


def base_kernel(x, weight, *outs):
    part, width = lax.axis_index("narrow"), outs[0].shape[1]
    for s, out in enumerate(outs):
        columns = pl.ds(pl.multiple_of((part ^ s) * width, width), width)

        def step(i, carry, out=out, columns=columns):
            at = pl.ds(pl.multiple_of(i * 256, 256), 256)
            out[at, :] = dot_nn(x[at, :], weight[:, columns])
            return carry

        lax.fori_loop(0, x.shape[0] // 256, step, 0, unroll=True)


def input_most_kernel(offsets, per_owner, parts, pieces, *refs):
    cots, (weight, mine, other, places, out, features) = refs[:parts], refs[parts:]
    part, width = lax.axis_index("narrow"), cots[0].shape[1]
    tile = 256
    values = whole(mine, other)
    for s, cot in enumerate(cots):
        columns = pl.ds(pl.multiple_of((part ^ s) * width, width), width)
        features[:, columns] = cot[...]
    for i in range(out.shape[0] // tile):
        at = pl.ds(i * tile, tile)
        here = values[:, i * tile : (i + 1) * tile]
        wide = [spread_tile(here, places[:, at], offset(), per_owner) for offset in offsets]
        term = dot_tn(jnp.concatenate(wide, axis=0), pieces[...])
        out[at, :] = dot_nt(features[at, :], weight[...]) + term


def input_last_kernel(offset, per_owner, piece, partial, mine, other, places, out):
    tile = 256
    values = whole(mine, other)
    for i in range(out.shape[0] // tile):
        at = pl.ds(i * tile, tile)
        wide = spread_tile(
            values[:, i * tile : (i + 1) * tile], places[:, at], offset(), per_owner
        )
        out[at, :] = (partial[at, :] + dot_tn(wide, piece[...])).astype(out.dtype)


def grad_down_kernel(from_a, from_b, term, out):
    tile = 64
    for i in range(out.shape[0] // tile):
        at = pl.ds(i * tile, tile)
        out[at, :] = term[at, :] + from_a[at, :].astype(F32) + from_b[at, :].astype(F32)


def projected_kernel(offsets, per_owner, *refs):
    ups = refs[: len(offsets)]
    base, mine, other, places, out = refs[len(offsets) :]
    values = whole(mine, other)
    tile = 256
    for i in range(out.shape[0] // tile):
        at = pl.ds(i * tile, tile)
        update = jnp.zeros((tile, out.shape[1]), F32)
        for offset, up in zip(offsets, ups):
            here = values[:, i * tile : (i + 1) * tile]
            update += dot_tn(spread_tile(here, places[:, at], offset(), per_owner), up[...])
        update = (ADAPTER_SCALE * update).astype(BF16).astype(F32)
        out[at, :] = (base[at, :] + update).astype(out.dtype)


def pair_lists(right_senders, left_senders):
    return [
        [(d, d + 1) for d in right_senders if d % 2 == odd]
        + [(d, d - 1) for d in left_senders if d % 2 != odd]
        for odd in (0, 1)
    ]


def shift(value, pairs):
    return lax.ppermute(value, "wide", pairs) if pairs else None


def swap_narrow(value, bit):
    size = lax.axis_size("narrow")
    return lax.ppermute(value, "narrow", [(d, d ^ bit) for d in range(size)])


def narrow_bits():
    size, bits = lax.axis_size("narrow"), []
    while 1 << len(bits) < size:
        bits.append(1 << len(bits))
    return bits


def sum_narrow(mine, other, scale, held=()):
    bits = narrow_bits()
    mine = mine + swap_narrow(other, bits[0])
    for bit in bits[1:]:
        mine = mine + swap_narrow(mine, bit)
    mine = (scale * mine).astype(BF16)
    other, *held = tie(swap_narrow(mine, bits[0]), *held)
    return (mine, other), held


def body(x, token_adapter_index, weight, down, up, cot):
    owners, me = lax.axis_size("wide"), lax.axis_index("wide")
    parts = lax.axis_size("narrow")
    per_owner, width_part, rank = down.shape
    value_part = up.shape[2]
    rows = per_owner * rank
    tokens = x.shape[0]
    adapters = owners * per_owner
    last = owners - 1
    down_own = jnp.swapaxes(down, 1, 2).reshape(rows, width_part)
    up_own = up.reshape(rows, value_part)
    places = token_adapter_index[:, 0][None, :] - me * per_owner
    places = jnp.where(places < 0, places + adapters, places)

    def fixed(offset):
        return lambda: offset

    def by_side(at_even, at_odd):
        return lambda: jnp.where(lax.axis_index("wide") % 2 == 0, at_even, at_odd)

    def arriving(step, even_from_right):
        def offset():
            me = lax.axis_index("wide")
            from_right = (me % 2 == 0) == even_from_right
            right = jnp.where(me + step < owners, step, -owners)
            left = jnp.where(me >= step, owners - step, -owners)
            return jnp.where(from_right, right, left)

        return offset

    def from_a(step):
        def valid():
            me = lax.axis_index("wide")
            return jnp.where(me % 2 == 0, me + step < owners, me >= step)

        return valid

    def gather_pairs(step):
        return pair_lists(range(step - 1, last), range(1, owners - step + 1))

    def reduce_pairs(step):
        return pair_lists(range(min(step, last)), range(max(owners - step, 1), owners))

    right, left = range(last), range(1, owners)
    pairs_a, pairs_b = pair_lists(right, left)

    def across(bits):
        def offset():
            me = lax.axis_index("wide")
            return (me ^ bits) - me + jnp.where((me ^ bits) < me, owners, 0)

        return offset

    up_all = [(up_own, fixed(0))] + [
        (shift(up_own, [(d ^ bits, d) for d in range(owners)]), across(bits))
        for bits in range(1, owners)
    ]
    got_b = shift(down_own, pairs_b)
    got_a = shift(down_own, pairs_a)
    low = pick("pick_own", [(down_own, fixed(0))], places, x, per_owner, flops=2 * 10**9)

    outs = [((tokens, value_part), F32)] * parts
    base = local_kernel("base", base_kernel, outs, x, weight, flops=3 * 10**9)
    cot_here, low, *base = tie(cot, low, *base)
    back = pick("pick_back", up_all, places, cot_here, per_owner, halved=True, flops=BACK_FLOPS)
    back, (got_a, got_b) = sum_narrow(*back, ADAPTER_SCALE, (got_a, got_b))

    (term_first,) = outer_terms(
        "terms_first", back, places, x, [by_side(owners - 1, 1)], [F32], per_owner, 1.0
    )
    offsets = [fixed(0)] + [by_side(owners - s, s) for s in range(2, owners)]
    terms = outer_terms("terms_rest", back, places, x, offsets, [F32] * len(offsets), per_owner, 1.0)
    terms = [terms[0], term_first, *terms[1:]]

    sums = dict(enumerate(base))
    cots = {0: cot}
    near_bit, *far_bits = narrow_bits()

    def send_base(bit):
        values = {s: sums.pop(s) for s in list(sums) if s & bit}
        return {
            s ^ bit: swap_narrow(v if bit == near_bit else v.astype(BF16), bit)
            for s, v in values.items()
        }

    def add_base(came):
        for s, value in came.items():
            sums[s] = sums[s] + value.astype(F32)

    def gather_cots(cots, bit):
        for s in list(cots):
            cots[s | bit] = swap_narrow(cots[s], bit)

    pieces = {}
    for step in range(1, owners):
        if step > 1:
            got_a, got_b, low = tie(got_a, got_b, low)
        gathers, reduces = gather_pairs(step + 1), reduce_pairs(step)
        sides = [
            (step, True, bool(gathers[0]), bool(reduces[0])),
            (step, False, bool(gathers[1]), bool(reduces[1])),
        ]
        if sides[0][3] and sides[1][3]:
            send_a, send_b = local_kernel(
                f"send_{step}",
                functools.partial(send_kernel, sides, owners),
                [(down_own.shape, BF16)] * 2,
                terms[step],
                terms[owners - step],
                late=[got_b, got_a],
            )
        else:
            send_a = got_b
            if sides[0][3]:
                (send_a,) = local_kernel(
                    f"send_{step}",
                    lambda came, term, out, sides=sides: send_kernel(
                        sides[:1], owners, came, came, term, term, out
                    ),
                    [(down_own.shape, BF16)],
                    terms[step],
                    late=[got_b],
                )
            send_b = got_a
        send_a, send_b, got_a, got_b = tie(send_a, send_b, got_a, got_b)
        if step == 2:
            send_a, send_b, *values = tie(send_a, send_b, *cots.values())
            cots = dict(zip(cots, values))
        if step == last:
            send_a, send_b, back_partial = tie(send_a, send_b, back_partial)
        live_a, live_b = gather_pairs(step)
        if live_a:
            pieces["a", step] = got_a
        if live_b:
            pieces["b", step] = got_b
        if step < last:
            arrived = [
                (pieces[side, step], arriving(step, side == "a"))
                for side in "ab"
                if (side, step) in pieces
            ]
        if 2 * step == owners:
            arrived = [((got_a, got_b, from_a(step)), by_side(step, owners - step))]
        elif step == last:
            arrived = [(got_a, arriving(step, True))]
        got_b = shift(send_b, pairs_b)
        got_a = shift(send_a, pairs_a)
        low = pick(
            f"pick_{step}", arrived, places, x, per_owner, low, step == last, flops=PICK_FLOPS
        )
        if step == last:
            add_base(base_came)
            *low, sums[0] = tie(*low, sums[0])
        elif step <= 2:
            after = term_first if step == 1 else low
            after, *values = tie(after, *sums.values())
            sums.update(zip(list(sums), values))
            if step == 1:
                base_came = send_base(near_bit)
                for bit in far_bits:
                    gather_cots(cots, bit)
            else:
                low = after
                add_base(base_came)
                for bit in far_bits[:-1]:
                    add_base(send_base(bit))
                base_came = send_base(far_bits[-1])
                gather_cots(cots, near_bit)
        if step == last - 1:
            gathered = [(down_own, fixed(0))]
            for k in range(1, last):
                a, b = pieces.get(("a", k)), pieces.get(("b", owners - k))
                piece = a if b is None else (a, b, from_a(k))
                gathered.append((piece, by_side(k, owners - k)))
            gathered.append((pieces["b", 1], by_side(last, 1)))
            (back_partial,) = local_kernel(
                "input_grad_most",
                functools.partial(input_most_kernel, [o for _, o in gathered], per_owner, parts),
                [((tokens, width_part), F32)],
                *[cots[s] for s in range(parts)],
                weight,
                *back,
                places,
                late=[d for d, _ in gathered],
                stacked=True,
                scratch=[pltpu.VMEM((tokens, parts * value_part), BF16)],
            )

    low, _ = sum_narrow(*low, 1.0)
    grad_up, *up_terms = outer_terms(
        "up_terms",
        low,
        places,
        cot,
        [fixed(m) for m in range(owners)],
        [F32] + [BF16] * last,
        per_owner,
        ADAPTER_SCALE,
    )
    places_late, *up_terms = tie(places, *up_terms)
    got_up = [
        shift(term, [(d, (d + m) % owners) for d in range(owners)])
        for m, term in enumerate(up_terms, 1)
    ]

    projected = local_kernel(
        "projected",
        functools.partial(projected_kernel, [o for _, o in up_all], per_owner),
        [((tokens, value_part), BF16)],
        sums[0],
        *low,
        places_late,
        late=[u for u, _ in up_all],
    )[0]
    (input_grad,) = local_kernel(
        "input_grad",
        functools.partial(input_last_kernel, arriving(last, True), per_owner),
        [((tokens, width_part), BF16)],
        back_partial,
        *back,
        places_late,
        late=[pieces["a", last]],
    )
    input_grad, projected, got_a, got_b = tie(input_grad, projected, got_a, got_b)
    (grad_down,) = local_kernel(
        "grad_down",
        grad_down_kernel,
        [((rows, width_part), F32)],
        terms[0],
        late=[got_a, got_b],
        flops=FILLER_FLOPS,
    )

    grad_down, *got_up = tie(grad_down, *got_up)
    for got in got_up:
        grad_up += got.astype(F32)
    return (
        projected,
        input_grad,
        jnp.swapaxes(grad_down.reshape(per_owner, rank, width_part), 1, 2),
        grad_up.reshape(per_owner, rank, value_part),
    )


def solution(mesh):
    in_specs = (
        P(("groups", "wide"), "narrow"),
        P(("groups", "wide"), None),
        P("narrow", None),
        P(("groups", "wide"), "narrow", None),
        P(("groups", "wide"), None, "narrow"),
        P(("groups", "wide"), "narrow"),
    )
    out_specs = (
        P(("groups", "wide"), "narrow"),
        P(("groups", "wide"), "narrow"),
        P(("groups", "wide"), "narrow", None),
        P(("groups", "wide"), None, "narrow"),
    )
    return jax.shard_map(body, mesh=mesh, in_specs=in_specs, out_specs=out_specs, check_vma=False)
```

```python
import functools

import jax
import jax.numpy as jnp
from jax import lax
from jax.experimental import pallas as pl
from jax.experimental.pallas import tpu as pltpu
from jax.sharding import PartitionSpec as P

ADAPTER_SCALE = 2.0
F32 = jnp.float32
BF16 = jnp.bfloat16
VMEM_BYTES = 16 * 1024 * 1024

BACK_FLOPS = 4 * 10**9
SLOT_FLOPS = 3 * 10**9
SEND_FLOPS = 0, 10**9


def dot_nn(left, right):
    return jnp.dot(left, right, preferred_element_type=F32)


def dot_nt(left, right):
    return lax.dot_general(left, right, (((1,), (1,)), ((), ())), preferred_element_type=F32)


def dot_tn(left, right):
    return lax.dot_general(left, right, (((0,), (0,)), ((), ())), preferred_element_type=F32)


def tie(*values):
    return lax.optimization_barrier(values)


def alternatives(entry):
    choice = entry[2] if isinstance(entry, tuple) else None
    arrays = entry[:2] if isinstance(entry, tuple) else (entry,)
    return [tuple(a) if isinstance(a, list) else (a,) for a in arrays], choice


def local_kernel(name, kernel, outs, *operands, late=(), flops=0, stacked=False, scratch=()):
    late = [alternatives(entry) for entry in late]
    sources = [array for blocks, _ in late for alternative in blocks for array in alternative]
    slots = [
        jax.ShapeDtypeStruct(
            (sum(a.shape[0] for a in blocks[0]), blocks[0][0].shape[1]), blocks[0][0].dtype
        )
        for blocks, _ in late
    ]
    chunks = [max(len(alternative) for alternative in blocks) for blocks, _ in late]

    def fetching(*refs):
        ins, refs = refs[: len(sources)], refs[len(sources) :]
        direct, refs = refs[: len(operands)], refs[len(operands) :]
        results, refs = refs[: len(outs)], refs[len(outs) :]
        extra, refs = refs[: len(scratch)], refs[len(scratch) :]
        semaphores = refs[-1]
        fetched = refs[:-1]
        if stacked:
            rows = slots[0].shape[0]
            fetched = [fetched[0].at[pl.ds(i * rows, rows)] for i in range(len(late))]
        ins, waits = iter(ins), []
        for (blocks, choice), slot, count in zip(late, fetched, chunks):
            first_semaphore, copies = len(waits), []
            size = slot.shape[0] // count
            for alternative in blocks:
                parts = [
                    source.at[pl.ds(start, size)] if block.shape[0] > size else source
                    for block, source in [(block, next(ins)) for block in alternative]
                    for start in range(0, block.shape[0], size)
                ]
                copies.append(
                    [
                        pltpu.make_async_copy(
                            part, slot.at[pl.ds(i * size, size)], semaphores.at[first_semaphore + i]
                        )
                        for i, part in enumerate(parts)
                    ]
                )
            if choice is None:
                for copy in copies[0]:
                    copy.start()
            else:
                first = choice()
                for one, two in zip(*copies):
                    pl.when(first)(one.start)
                    pl.when(jnp.logical_not(first))(two.start)
            waits += copies[0]
        for copy in waits:
            copy.wait()
        kernel(*(refs[:1] if stacked else fetched), *direct, *results, *extra)

    buffers = [pltpu.VMEM(slot.shape, slot.dtype) for slot in slots]
    if stacked:
        rows, columns = slots[0].shape
        buffers = [pltpu.VMEM((len(slots) * rows, columns), slots[0].dtype)]
    return pl.pallas_call(
        fetching if late else kernel,
        name=name,
        out_shape=[jax.ShapeDtypeStruct(s, t) for s, t in outs],
        in_specs=[pl.BlockSpec(memory_space=pl.ANY)] * len(sources)
        + [pl.BlockSpec(memory_space=pltpu.VMEM)] * len(operands),
        out_specs=[pl.BlockSpec(memory_space=pltpu.VMEM)] * len(outs),
        scratch_shapes=[
            *scratch,
            *buffers,
            *([pltpu.SemaphoreType.DMA((sum(chunks),))] if late else []),
        ],
        compiler_params=pltpu.CompilerParams(vmem_limit_bytes=VMEM_BYTES),
        cost_estimate=pl.CostEstimate(flops=flops, bytes_accessed=0, transcendentals=0),
    )(*sources, *operands)


def tile_of(extent):
    return 256 if extent % 256 == 0 else 128


def spread_tile(values, places, offset, per_owner):
    return jnp.concatenate(
        [
            jnp.where(places == offset * per_owner + a, values, jnp.zeros((), values.dtype))
            for a in range(per_owner)
        ],
        axis=0,
    )


def pick_kernel(offsets, per_owner, has_start, halved, *refs):
    count = len(offsets)
    pieces, (places, rhs), rest = refs[:count], refs[count : count + 2], refs[count + 2 :]
    start, outs = (rest[0], rest[1:]) if has_start else (None, rest)
    tokens = rhs.shape[0]
    tile = tile_of(tokens)
    rank = pieces[0].shape[0] // per_owner
    core = lax.axis_index("narrow") % 2
    for i in range(tokens // tile):
        at = pl.ds(i * tile, tile)
        here, right = places[:, at], rhs[at, :]
        total = jnp.zeros((rank, tile), F32) if start is None else start[:, at]
        for piece, offset in zip(pieces, offsets):
            products = dot_nt(piece[...], right)
            for a in range(per_owner):
                total += jnp.where(
                    here == offset() * per_owner + a, products[a * rank : (a + 1) * rank], 0.0
                )
        if halved:
            low, high = total[: rank // 2], total[rank // 2 :]
            outs[0][:, at] = jnp.where(core == 0, low, high)
            outs[1][:, at] = jnp.where(core == 0, high, low)
        else:
            outs[0][:, at] = total


def pick(name, pieces, places, rhs, per_owner, start=None, halved=False, flops=0):
    rows = sum(block.shape[0] for block in alternatives(pieces[0][0])[0][0])
    rank, tokens = rows // per_owner, rhs.shape[0]
    kernel = functools.partial(
        pick_kernel, [o for _, o in pieces], per_owner, start is not None, halved
    )
    more = [] if start is None else [start]
    outs = [((rank // 2, tokens), F32)] * 2 if halved else [((rank, tokens), F32)]
    outs = local_kernel(
        name, kernel, outs, places, rhs, *more, late=[p for p, _ in pieces], flops=flops
    )
    return outs if halved else outs[0]


def whole(mine, other):
    first = lax.axis_index("narrow") % 2 == 0
    return jnp.concatenate(
        [jnp.where(first, mine[...], other[...]), jnp.where(first, other[...], mine[...])], axis=0
    )


def terms_kernel(offsets, per_owner, scale, other, mine, places, rhs, *outs):
    tile = tile_of(rhs.shape[1])
    values = whole(mine, other)
    for offset, out in zip(offsets, outs):
        wide = spread_tile(values, places[...], offset(), per_owner)

        def step(i, carry, wide=wide, out=out):
            at = pl.ds(pl.multiple_of(i * tile, tile), tile)
            out[:, at] = (scale * dot_nn(wide, rhs[:, at])).astype(out.dtype)
            return carry

        lax.fori_loop(0, rhs.shape[1] // tile, step, 0, unroll=True)


def outer_terms(name, values, places, rhs, offsets, types, per_owner, scale):
    mine, other = values
    shape = (2 * mine.shape[0] * per_owner, rhs.shape[1])
    kernel = functools.partial(terms_kernel, offsets, per_owner, scale)
    return local_kernel(
        name, kernel, [(shape, t) for t in types], mine, places, rhs, late=[other]
    )


def send_kernel(sides, owners, start, *refs):
    me = lax.axis_index("wide")
    got, terms, outs = refs[:2], refs[2:4], refs[4:]
    blocks, tile = len(outs) // 2, 64
    for side, (step, even_to_right, moving, summing) in enumerate(sides):
        to_right = (me % 2 == 0) == even_to_right
        passes_on = jnp.where(to_right, me >= step, me + step < owners)
        came, term, begin = got[side], terms[side], 0
        for out in outs[side * blocks : (side + 1) * blocks]:
            for i in range(out.shape[0] // tile):
                at = pl.ds(begin + i * tile, tile)
                value = came[at, :]
                if summing:
                    here = term[pl.ds(start + begin + i * tile, tile), :]
                    total = (here + value.astype(F32)).astype(BF16)
                    value = jnp.where(passes_on, value, total) if moving else total
                out[pl.ds(i * tile, tile), :] = value
            begin += out.shape[0]


def base_kernel(parts, x, weight, keep, give):
    part, width, rows = lax.axis_index("narrow"), keep.shape[1], x.shape[0]
    for s in range(parts):
        columns = pl.ds(pl.multiple_of((part ^ s) * width, width), width)
        out, start = (keep, give)[s % 2], s // 2 * rows
        for i in range(rows // 256):
            out[pl.ds(start + i * 256, 256), :] = dot_nn(
                x[pl.ds(i * 256, 256), :], weight[:, columns]
            )


def base_back_kernel(parts, *refs):
    cots, (weight, early, out, features) = refs[:parts], refs[parts:]
    part, width = lax.axis_index("narrow"), cots[0].shape[1]
    tile = 256
    for s, cot in enumerate(cots):
        columns = pl.ds(pl.multiple_of((part ^ s) * width, width), width)
        features[:, columns] = cot[...]
    for i in range(out.shape[0] // tile):
        at = pl.ds(i * tile, tile)
        out[at, :] = early[at, :] + dot_nt(features[at, :], weight[...])


def input_early_kernel(offsets, per_owner, pieces, mine, other, places, out):
    tile = 256
    values = whole(mine, other)
    for i in range(out.shape[0] // tile):
        at = pl.ds(i * tile, tile)
        here = values[:, i * tile : (i + 1) * tile]
        wide = [spread_tile(here, places[:, at], offset(), per_owner) for offset in offsets]
        out[at, :] = dot_tn(jnp.concatenate(wide, axis=0), pieces[...])


def input_grad_kernel(offsets, per_owner, pieces, base, mine, other, places, out):
    tile = 256
    values = whole(mine, other)
    for i in range(out.shape[0] // tile):
        at = pl.ds(i * tile, tile)
        here = values[:, i * tile : (i + 1) * tile]
        wide = [spread_tile(here, places[:, at], offset(), per_owner) for offset in offsets]
        term = dot_tn(jnp.concatenate(wide, axis=0), pieces[...])
        out[at, :] = (base[at, :] + term).astype(out.dtype)


def grad_down_kernel(from_a, from_b, term, out):
    tile = 64
    for i in range(out.shape[0] // tile):
        at = pl.ds(i * tile, tile)
        out[at, :] = term[at, :] + from_a[at, :].astype(F32) + from_b[at, :].astype(F32)


def projected_kernel(offsets, per_owner, *refs):
    ups = refs[: len(offsets)]
    base, more, mine, other, places, out = refs[len(offsets) :]
    values = whole(mine, other)
    tile = 256
    for i in range(out.shape[0] // tile):
        at = pl.ds(i * tile, tile)
        update = jnp.zeros((tile, out.shape[1]), F32)
        for offset, up in zip(offsets, ups):
            here = values[:, i * tile : (i + 1) * tile]
            update += dot_tn(spread_tile(here, places[:, at], offset(), per_owner), up[...])
        update = (ADAPTER_SCALE * update).astype(BF16).astype(F32)
        out[at, :] = (base[at, :] + more[at, :].astype(F32) + update).astype(out.dtype)


def pair_lists(right_senders, left_senders):
    return [
        [(d, d + 1) for d in right_senders if d % 2 == odd]
        + [(d, d - 1) for d in left_senders if d % 2 != odd]
        for odd in (0, 1)
    ]


def shift(value, pairs):
    return lax.ppermute(value, "wide", pairs) if pairs else None


def swap_narrow(value, bit):
    size = lax.axis_size("narrow")
    return lax.ppermute(value, "narrow", [(d, d ^ bit) for d in range(size)])


def narrow_bits():
    size, bits = lax.axis_size("narrow"), []
    while 1 << len(bits) < size:
        bits.append(1 << len(bits))
    return bits


def sum_narrow(mine, other, scale, core=(), during=None, chips=(), end=()):
    bits = narrow_bits()
    mine = mine + swap_narrow(other, bits[0])
    mine, *core = tie(mine, *core)
    if during is not None:
        chips = (*chips, *during(*core))
    for bit in bits[1:]:
        mine = mine + swap_narrow(mine, bit)
    mine, *chips = tie(mine, *chips)
    mine = (scale * mine).astype(BF16)
    other, *end = tie(swap_narrow(mine, bits[0]), *end)
    return (mine, other), core, chips, end


def body(x, token_adapter_index, weight, down, up, cot):
    owners, me = lax.axis_size("wide"), lax.axis_index("wide")
    parts = lax.axis_size("narrow")
    per_owner, width_part, rank = down.shape
    value_part = up.shape[2]
    rows = per_owner * rank
    tokens = x.shape[0]
    adapters = owners * per_owner
    last = owners - 1
    down_own = jnp.swapaxes(down, 1, 2).reshape(rows, width_part)
    up_own = up.reshape(rows, value_part)
    places = token_adapter_index[:, 0][None, :] - me * per_owner
    places = jnp.where(places < 0, places + adapters, places)

    def fixed(offset):
        return lambda: offset

    def by_side(at_even, at_odd):
        return lambda: jnp.where(lax.axis_index("wide") % 2 == 0, at_even, at_odd)

    def arriving(step, even_from_right):
        def offset():
            me = lax.axis_index("wide")
            from_right = (me % 2 == 0) == even_from_right
            right = jnp.where(me + step < owners, step, -owners)
            left = jnp.where(me >= step, owners - step, -owners)
            return jnp.where(from_right, right, left)

        return offset

    def from_a(step):
        def valid():
            me = lax.axis_index("wide")
            return jnp.where(me % 2 == 0, me + step < owners, me >= step)

        return valid

    def gather_pairs(step):
        return pair_lists(range(step - 1, last), range(1, owners - step + 1))

    def reduce_pairs(step):
        return pair_lists(range(min(step, last)), range(max(owners - step, 1), owners))

    right, left = range(last), range(1, owners)
    pairs_a, pairs_b = pair_lists(right, left)

    def across(bits):
        def offset():
            me = lax.axis_index("wide")
            return (me ^ bits) - me + jnp.where((me ^ bits) < me, owners, 0)

        return offset

    up_all = [(up_own, fixed(0))] + [
        (shift(up_own, [(d ^ bits, d) for d in range(owners)]), across(bits))
        for bits in range(1, owners)
    ]
    got_b = shift(down_own, pairs_b)
    got_a = shift(down_own, pairs_a)
    low = pick("pick_own", [(down_own, fixed(0))], places, x, per_owner, flops=2 * 10**9)

    near_bit, *far_bits = narrow_bits()

    def base_products(x):
        return local_kernel(
            "base",
            functools.partial(base_kernel, parts),
            [((parts // 2 * tokens, value_part), F32)] * 2,
            x,
            weight,
        )

    cot_here, low = tie(cot, low)
    back = pick("pick_back", up_all, places, cot_here, per_owner, halved=True, flops=BACK_FLOPS)
    back_mine, cot_near = tie(back[0], cot)
    back, cot_near = (back_mine, back[1]), swap_narrow(cot_near, near_bit)
    back, _, (base_keep, base_give), _ = sum_narrow(
        *back, ADAPTER_SCALE, core=(x,), during=base_products
    )

    offsets = [fixed(0)] + [by_side(owners - s, s) for s in range(1, owners)]
    terms = outer_terms("terms", back, places, x, offsets, [F32] * owners, per_owner, 1.0)
    *terms, got_a, got_b = tie(*terms, got_a, got_b)

    half = rows // 2
    got_a, got_b, pieces = [got_a], [got_b], {}
    for step in range(1, owners):
        gathers, reduces = gather_pairs(step + 1), reduce_pairs(step)
        live_a, live_b = gather_pairs(step)
        sides = [
            (step, True, bool(gathers[0]), bool(reduces[0])),
            (step, False, bool(gathers[1]), bool(reduces[1])),
        ]
        next_a, next_b = [], []
        for h in range(len(got_a)):
            if step == 2 and h == 1:
                got_a[h], got_b[h], low = tie(got_a[h], got_b[h], low)
            elif step > 2 and h == 1:
                got_a[h], got_b[h], low = tie(got_a[h], got_b[h], low)
            if step == 2 and h == 0:
                got_a[h], got_b[h], _ = tie(got_a[h], got_b[h], base_sum)
            if step == last and h == 0:
                got_a[h], got_b[h], early = tie(got_a[h], got_b[h], early)
            outs = [((half, width_part), BF16)] * (2 * (2 // len(got_a)))
            sends = local_kernel(
                f"send_{step}_{h}",
                functools.partial(send_kernel, sides, owners, h * half),
                outs,
                terms[step],
                terms[owners - step] if sides[1][3] else terms[step],
                late=[got_b[h], got_a[h]],
                flops=SEND_FLOPS[h],
            )
            *sends, got_a[h], got_b[h], x_late, places_here = tie(
                *sends, got_a[h], got_b[h], x, places
            )
            if step > 1 and h == 0:
                low = pick(
                    f"pick_{step - 1}", arrived, places, x_late, per_owner, low, flops=SLOT_FLOPS
                )
            if step == 1:
                base_give, cot_here, _ = tie(base_give, cot, sends[0])
                base_sum = base_keep + swap_narrow(base_give, near_bit)
                cots = {0: cot_here, near_bit: cot_near}
                for bit in far_bits:
                    block = swap_narrow(jnp.concatenate(list(cots.values()), axis=0), bit)
                    for i, s in enumerate(list(cots)):
                        cots[s | bit] = block[i * tokens : (i + 1) * tokens]
            if step == last - 1 and h == 1:
                near = [(down_own, fixed(0)), (pieces["a", 1], by_side(1, last))]
                near.append((pieces["b", 1], by_side(last, 1)))
                (early,) = local_kernel(
                    "input_early",
                    functools.partial(input_early_kernel, [o for _, o in near], per_owner),
                    [((tokens, width_part), F32)],
                    *back,
                    places_here,
                    late=[d for d, _ in near],
                    stacked=True,
                )
            for i in range(len(sends) // 2):
                next_b.append(shift(sends[len(sends) // 2 + i], pairs_b))
                next_a.append(shift(sends[i], pairs_a))
        if live_a:
            pieces["a", step] = got_a
        if live_b:
            pieces["b", step] = got_b
        arrived = [
            (pieces[side, step], arriving(step, side == "a"))
            for side in "ab"
            if (side, step) in pieces
        ]
        if 2 * step == owners:
            arrived = [((got_a, got_b, from_a(step)), by_side(step, owners - step))]
        got_a, got_b = next_a, next_b
    low = pick(f"pick_{last}", arrived, places, x, per_owner, low, True)
    *low, got_a[0], got_b[0] = tie(*low, got_a[0], got_b[0])


    def base_product(*held):
        cots.update(zip(cots, held[1:]))
        return local_kernel(
            "base_back",
            functools.partial(base_back_kernel, parts),
            [((tokens, width_part), F32)],
            *[cots[s] for s in range(parts)],
            weight,
            held[0],
            scratch=[pltpu.VMEM((tokens, parts * value_part), BF16)],
        )

    low, _, (got_a[1], got_b[1], base_back), _ = sum_narrow(
        *low,
        1.0,
        core=(early, *cots.values()),
        during=base_product,
        chips=(got_a[1], got_b[1]),
    )
    base_sum, _ = tie(base_sum, low[0])
    sums = {2 * i: base_sum[i * tokens : (i + 1) * tokens] for i in range(parts // 2)}
    for bit in far_bits[:-1]:
        for s in [s for s in sums if s & bit]:
            got = swap_narrow(sums.pop(s).astype(BF16), bit)
            sums[s ^ bit] = sums[s ^ bit] + got.astype(F32)
    base_came = swap_narrow(sums[far_bits[-1]].astype(BF16), far_bits[-1])
    grad_up, *up_terms = outer_terms(
        "up_terms",
        low,
        places,
        cot,
        [fixed(m) for m in range(owners)],
        [F32] + [BF16] * last,
        per_owner,
        ADAPTER_SCALE,
    )
    places_late, *up_terms = tie(places, *up_terms)
    got_up = [
        shift(term, [(d, (d + m) % owners) for d in range(owners)])
        for m, term in enumerate(up_terms, 1)
    ]

    projected = local_kernel(
        "projected",
        functools.partial(projected_kernel, [o for _, o in up_all], per_owner),
        [((tokens, value_part), BF16)],
        sums[0],
        base_came,
        *low,
        places_late,
        late=[u for u, _ in up_all],
    )[0]
    slots = [(pieces["a", last], arriving(last, True))]
    for step in range(2, last):
        a, b = pieces.get(("a", step)), pieces.get(("b", owners - step))
        slots.append(((a, b, from_a(step)) if b is not None else a, by_side(step, owners - step)))
    (input_grad,) = local_kernel(
        "input_grad",
        functools.partial(input_grad_kernel, [o for _, o in slots], per_owner),
        [((tokens, width_part), BF16)],
        base_back,
        *back,
        places_late,
        late=[d for d, _ in slots],
        stacked=True,
    )
    (grad_down,) = local_kernel(
        "grad_down",
        grad_down_kernel,
        [((rows, width_part), F32)],
        terms[0],
        late=[got_a, got_b],
    )

    grad_down, input_grad, projected, *got_up = tie(grad_down, input_grad, projected, *got_up)
    for got in got_up:
        grad_up += got.astype(F32)
    return (
        projected,
        input_grad,
        jnp.swapaxes(grad_down.reshape(per_owner, rank, width_part), 1, 2),
        grad_up.reshape(per_owner, rank, value_part),
    )


def solution(mesh):
    in_specs = (
        P(("groups", "wide"), "narrow"),
        P(("groups", "wide"), None),
        P("narrow", None),
        P(("groups", "wide"), "narrow", None),
        P(("groups", "wide"), None, "narrow"),
        P(("groups", "wide"), "narrow"),
    )
    out_specs = (
        P(("groups", "wide"), "narrow"),
        P(("groups", "wide"), "narrow"),
        P(("groups", "wide"), "narrow", None),
        P(("groups", "wide"), None, "narrow"),
    )
    return jax.shard_map(body, mesh=mesh, in_specs=in_specs, out_specs=out_specs, check_vma=False)
```

```python
import functools

import jax
import jax.numpy as jnp
from jax import lax
from jax.experimental import pallas as pl
from jax.experimental.pallas import tpu as pltpu
from jax.sharding import PartitionSpec as P

ADAPTER_SCALE = 2.0
F32 = jnp.float32
BF16 = jnp.bfloat16
VMEM_BYTES = 16 * 1024 * 1024

BACK_FLOPS = 4 * 10**9
SLOT_FLOPS = 3 * 10**9
SEND_FLOPS = 0, 10**9


def dot_nn(left, right):
    return jnp.dot(left, right, preferred_element_type=F32)


def dot_nt(left, right):
    return lax.dot_general(left, right, (((1,), (1,)), ((), ())), preferred_element_type=F32)


def dot_tn(left, right):
    return lax.dot_general(left, right, (((0,), (0,)), ((), ())), preferred_element_type=F32)


def tie(*values):
    return lax.optimization_barrier(values)


def alternatives(entry):
    choice = entry[2] if isinstance(entry, tuple) else None
    arrays = entry[:2] if isinstance(entry, tuple) else (entry,)
    return [tuple(a) if isinstance(a, list) else (a,) for a in arrays], choice


def local_kernel(name, kernel, outs, *operands, late=(), flops=0, stacked=False, scratch=()):
    late = [alternatives(entry) for entry in late]
    sources = [array for blocks, _ in late for alternative in blocks for array in alternative]
    slots = [
        jax.ShapeDtypeStruct(
            (sum(a.shape[0] for a in blocks[0]), blocks[0][0].shape[1]), blocks[0][0].dtype
        )
        for blocks, _ in late
    ]
    chunks = [max(len(alternative) for alternative in blocks) for blocks, _ in late]

    def fetching(*refs):
        ins, refs = refs[: len(sources)], refs[len(sources) :]
        direct, refs = refs[: len(operands)], refs[len(operands) :]
        results, refs = refs[: len(outs)], refs[len(outs) :]
        extra, refs = refs[: len(scratch)], refs[len(scratch) :]
        semaphores = refs[-1]
        fetched = refs[:-1]
        if stacked:
            rows = slots[0].shape[0]
            fetched = [fetched[0].at[pl.ds(i * rows, rows)] for i in range(len(late))]
        ins, waits = iter(ins), []
        for (blocks, choice), slot, count in zip(late, fetched, chunks):
            first_semaphore, copies = len(waits), []
            size = slot.shape[0] // count
            for alternative in blocks:
                parts = [
                    source.at[pl.ds(start, size)] if block.shape[0] > size else source
                    for block, source in [(block, next(ins)) for block in alternative]
                    for start in range(0, block.shape[0], size)
                ]
                copies.append(
                    [
                        pltpu.make_async_copy(
                            part, slot.at[pl.ds(i * size, size)], semaphores.at[first_semaphore + i]
                        )
                        for i, part in enumerate(parts)
                    ]
                )
            if choice is None:
                for copy in copies[0]:
                    copy.start()
            else:
                first = choice()
                for one, two in zip(*copies):
                    pl.when(first)(one.start)
                    pl.when(jnp.logical_not(first))(two.start)
            waits += copies[0]
        for copy in waits:
            copy.wait()
        kernel(*(refs[:1] if stacked else fetched), *direct, *results, *extra)

    buffers = [pltpu.VMEM(slot.shape, slot.dtype) for slot in slots]
    if stacked:
        rows, columns = slots[0].shape
        buffers = [pltpu.VMEM((len(slots) * rows, columns), slots[0].dtype)]
    return pl.pallas_call(
        fetching if late else kernel,
        name=name,
        out_shape=[jax.ShapeDtypeStruct(s, t) for s, t in outs],
        in_specs=[pl.BlockSpec(memory_space=pl.ANY)] * len(sources)
        + [pl.BlockSpec(memory_space=pltpu.VMEM)] * len(operands),
        out_specs=[pl.BlockSpec(memory_space=pltpu.VMEM)] * len(outs),
        scratch_shapes=[
            *scratch,
            *buffers,
            *([pltpu.SemaphoreType.DMA((sum(chunks),))] if late else []),
        ],
        compiler_params=pltpu.CompilerParams(vmem_limit_bytes=VMEM_BYTES),
        cost_estimate=pl.CostEstimate(flops=flops, bytes_accessed=0, transcendentals=0),
    )(*sources, *operands)


def tile_of(extent):
    return 256 if extent % 256 == 0 else 128


def spread_tile(values, places, offset, per_owner):
    return jnp.concatenate(
        [
            jnp.where(places == offset * per_owner + a, values, jnp.zeros((), values.dtype))
            for a in range(per_owner)
        ],
        axis=0,
    )


def pick_kernel(offsets, per_owner, has_start, halved, *refs):
    count = len(offsets)
    pieces, (places, rhs), rest = refs[:count], refs[count : count + 2], refs[count + 2 :]
    start, outs = (rest[0], rest[1:]) if has_start else (None, rest)
    tokens = rhs.shape[0]
    tile = tile_of(tokens)
    rank = pieces[0].shape[0] // per_owner
    core = lax.axis_index("narrow") % 2
    for i in range(tokens // tile):
        at = pl.ds(i * tile, tile)
        here, right = places[:, at], rhs[at, :]
        total = jnp.zeros((rank, tile), F32) if start is None else start[:, at]
        for piece, offset in zip(pieces, offsets):
            products = dot_nt(piece[...], right)
            for a in range(per_owner):
                total += jnp.where(
                    here == offset() * per_owner + a, products[a * rank : (a + 1) * rank], 0.0
                )
        if halved:
            low, high = total[: rank // 2], total[rank // 2 :]
            outs[0][:, at] = jnp.where(core == 0, low, high)
            outs[1][:, at] = jnp.where(core == 0, high, low)
        else:
            outs[0][:, at] = total


def pick(name, pieces, places, rhs, per_owner, start=None, halved=False, flops=0):
    rows = sum(block.shape[0] for block in alternatives(pieces[0][0])[0][0])
    rank, tokens = rows // per_owner, rhs.shape[0]
    kernel = functools.partial(
        pick_kernel, [o for _, o in pieces], per_owner, start is not None, halved
    )
    more = [] if start is None else [start]
    outs = [((rank // 2, tokens), F32)] * 2 if halved else [((rank, tokens), F32)]
    outs = local_kernel(
        name, kernel, outs, places, rhs, *more, late=[p for p, _ in pieces], flops=flops
    )
    return outs if halved else outs[0]


def whole(mine, other):
    first = lax.axis_index("narrow") % 2 == 0
    return jnp.concatenate(
        [jnp.where(first, mine[...], other[...]), jnp.where(first, other[...], mine[...])], axis=0
    )


def terms_kernel(offsets, per_owner, scale, other, mine, places, rhs, *outs):
    tile = tile_of(rhs.shape[1])
    values = whole(mine, other)
    for offset, out in zip(offsets, outs):
        wide = spread_tile(values, places[...], offset(), per_owner)

        def step(i, carry, wide=wide, out=out):
            at = pl.ds(pl.multiple_of(i * tile, tile), tile)
            out[:, at] = (scale * dot_nn(wide, rhs[:, at])).astype(out.dtype)
            return carry

        lax.fori_loop(0, rhs.shape[1] // tile, step, 0, unroll=True)


def outer_terms(name, values, places, rhs, offsets, types, per_owner, scale):
    mine, other = values
    shape = (2 * mine.shape[0] * per_owner, rhs.shape[1])
    kernel = functools.partial(terms_kernel, offsets, per_owner, scale)
    return local_kernel(
        name, kernel, [(shape, t) for t in types], mine, places, rhs, late=[other]
    )


def send_kernel(sides, owners, start, *refs):
    me = lax.axis_index("wide")
    got, terms, outs = refs[:2], refs[2:4], refs[4:]
    blocks, tile = len(outs) // 2, 64
    for side, (step, even_to_right, moving, summing) in enumerate(sides):
        to_right = (me % 2 == 0) == even_to_right
        passes_on = jnp.where(to_right, me >= step, me + step < owners)
        came, term, begin = got[side], terms[side], 0
        for out in outs[side * blocks : (side + 1) * blocks]:
            for i in range(out.shape[0] // tile):
                at = pl.ds(begin + i * tile, tile)
                value = came[at, :]
                if summing:
                    here = term[pl.ds(start + begin + i * tile, tile), :]
                    total = (here + value.astype(F32)).astype(BF16)
                    value = jnp.where(passes_on, value, total) if moving else total
                out[pl.ds(i * tile, tile), :] = value
            begin += out.shape[0]


def base_kernel(parts, x, weight, keep, give):
    part, width, rows = lax.axis_index("narrow"), keep.shape[1], x.shape[0]
    for s in range(parts):
        columns = pl.ds(pl.multiple_of((part ^ s) * width, width), width)
        out, start = (keep, give)[s % 2], s // 2 * rows
        for i in range(rows // 256):
            out[pl.ds(start + i * 256, 256), :] = dot_nn(
                x[pl.ds(i * 256, 256), :], weight[:, columns]
            )


def base_back_kernel(parts, *refs):
    cots, (weight, early, out, features) = refs[:parts], refs[parts:]
    part, width = lax.axis_index("narrow"), cots[0].shape[1]
    tile = 256
    for s, cot in enumerate(cots):
        columns = pl.ds(pl.multiple_of((part ^ s) * width, width), width)
        features[:, columns] = cot[...]
    for i in range(out.shape[0] // tile):
        at = pl.ds(i * tile, tile)
        out[at, :] = early[at, :] + dot_nt(features[at, :], weight[...])


def input_early_kernel(offsets, per_owner, pieces, mine, other, places, out):
    tile = 256
    values = whole(mine, other)
    for i in range(out.shape[0] // tile):
        at = pl.ds(i * tile, tile)
        here = values[:, i * tile : (i + 1) * tile]
        wide = [spread_tile(here, places[:, at], offset(), per_owner) for offset in offsets]
        out[at, :] = dot_tn(jnp.concatenate(wide, axis=0), pieces[...])


def input_grad_kernel(offsets, per_owner, pieces, base, mine, other, places, out):
    tile = 256
    values = whole(mine, other)
    for i in range(out.shape[0] // tile):
        at = pl.ds(i * tile, tile)
        here = values[:, i * tile : (i + 1) * tile]
        wide = [spread_tile(here, places[:, at], offset(), per_owner) for offset in offsets]
        term = dot_tn(jnp.concatenate(wide, axis=0), pieces[...])
        out[at, :] = (base[at, :] + term).astype(out.dtype)


def grad_down_kernel(from_a, from_b, term, out):
    tile = 64
    for i in range(out.shape[0] // tile):
        at = pl.ds(i * tile, tile)
        out[at, :] = term[at, :] + from_a[at, :].astype(F32) + from_b[at, :].astype(F32)


def projected_kernel(offsets, per_owner, *refs):
    ups = refs[: len(offsets)]
    base, more, mine, other, places, out = refs[len(offsets) :]
    values = whole(mine, other)
    tile = 256
    for i in range(out.shape[0] // tile):
        at = pl.ds(i * tile, tile)
        update = jnp.zeros((tile, out.shape[1]), F32)
        for offset, up in zip(offsets, ups):
            here = values[:, i * tile : (i + 1) * tile]
            update += dot_tn(spread_tile(here, places[:, at], offset(), per_owner), up[...])
        update = (ADAPTER_SCALE * update).astype(BF16).astype(F32)
        out[at, :] = (base[at, :] + more[at, :].astype(F32) + update).astype(out.dtype)


def pair_lists(right_senders, left_senders):
    return [
        [(d, d + 1) for d in right_senders if d % 2 == odd]
        + [(d, d - 1) for d in left_senders if d % 2 != odd]
        for odd in (0, 1)
    ]


def shift(value, pairs):
    return lax.ppermute(value, "wide", pairs) if pairs else None


def swap_narrow(value, bit):
    size = lax.axis_size("narrow")
    return lax.ppermute(value, "narrow", [(d, d ^ bit) for d in range(size)])


def narrow_bits():
    size, bits = lax.axis_size("narrow"), []
    while 1 << len(bits) < size:
        bits.append(1 << len(bits))
    return bits


def sum_narrow(mine, other, scale, core=(), during=None, chips=(), end=()):
    bits = narrow_bits()
    mine = mine + swap_narrow(other, bits[0])
    mine, *core = tie(mine, *core)
    if during is not None:
        chips = (*chips, *during(*core))
    for bit in bits[1:]:
        mine = mine + swap_narrow(mine, bit)
    mine, *chips = tie(mine, *chips)
    mine = (scale * mine).astype(BF16)
    other, *end = tie(swap_narrow(mine, bits[0]), *end)
    return (mine, other), core, chips, end


def body(x, token_adapter_index, weight, down, up, cot):
    owners, me = lax.axis_size("wide"), lax.axis_index("wide")
    parts = lax.axis_size("narrow")
    per_owner, width_part, rank = down.shape
    value_part = up.shape[2]
    rows = per_owner * rank
    tokens = x.shape[0]
    adapters = owners * per_owner
    last = owners - 1
    down_own = jnp.swapaxes(down, 1, 2).reshape(rows, width_part)
    up_own = up.reshape(rows, value_part)
    places = token_adapter_index[:, 0][None, :] - me * per_owner
    places = jnp.where(places < 0, places + adapters, places)

    def fixed(offset):
        return lambda: offset

    def by_side(at_even, at_odd):
        return lambda: jnp.where(lax.axis_index("wide") % 2 == 0, at_even, at_odd)

    def arriving(step, even_from_right):
        def offset():
            me = lax.axis_index("wide")
            from_right = (me % 2 == 0) == even_from_right
            right = jnp.where(me + step < owners, step, -owners)
            left = jnp.where(me >= step, owners - step, -owners)
            return jnp.where(from_right, right, left)

        return offset

    def from_a(step):
        def valid():
            me = lax.axis_index("wide")
            return jnp.where(me % 2 == 0, me + step < owners, me >= step)

        return valid

    def gather_pairs(step):
        return pair_lists(range(step - 1, last), range(1, owners - step + 1))

    def reduce_pairs(step):
        return pair_lists(range(min(step, last)), range(max(owners - step, 1), owners))

    right, left = range(last), range(1, owners)
    pairs_a, pairs_b = pair_lists(right, left)

    def across(bits):
        def offset():
            me = lax.axis_index("wide")
            return (me ^ bits) - me + jnp.where((me ^ bits) < me, owners, 0)

        return offset

    up_all = [(up_own, fixed(0))] + [
        (shift(up_own, [(d ^ bits, d) for d in range(owners)]), across(bits))
        for bits in range(1, owners)
    ]
    got_b = shift(down_own, pairs_b)
    got_a = shift(down_own, pairs_a)
    low = pick("pick_own", [(down_own, fixed(0))], places, x, per_owner, flops=2 * 10**9)

    near_bit, *far_bits = narrow_bits()

    def base_products(x):
        return local_kernel(
            "base",
            functools.partial(base_kernel, parts),
            [((parts // 2 * tokens, value_part), F32)] * 2,
            x,
            weight,
        )

    cot_here, low = tie(cot, low)
    back = pick("pick_back", up_all, places, cot_here, per_owner, halved=True, flops=BACK_FLOPS)
    back_mine, cot_near = tie(back[0], cot)
    back, cot_near = (back_mine, back[1]), swap_narrow(cot_near, near_bit)
    back, _, (base_keep, base_give), _ = sum_narrow(
        *back, ADAPTER_SCALE, core=(x,), during=base_products
    )

    offsets = [by_side(owners - s, s) for s in range(1, owners)]
    terms = outer_terms("terms", back, places, x, offsets, [F32] * last, per_owner, 1.0)
    *terms, got_a, got_b = tie(*terms, got_a, got_b)
    terms = [None, *terms]

    half = rows // 2
    got_a, got_b, pieces = [got_a], [got_b], {}
    for step in range(1, owners):
        gathers, reduces = gather_pairs(step + 1), reduce_pairs(step)
        live_a, live_b = gather_pairs(step)
        sides = [
            (step, True, bool(gathers[0]), bool(reduces[0])),
            (step, False, bool(gathers[1]), bool(reduces[1])),
        ]
        next_a, next_b = [], []
        for h in range(len(got_a)):
            if step == 2 and h == 1:
                got_a[h], got_b[h], low = tie(got_a[h], got_b[h], low)
            elif step > 2 and h == 1:
                got_a[h], got_b[h], low = tie(got_a[h], got_b[h], low)
            if step == 2 and h == 0:
                got_a[h], got_b[h], terms[0], base_sum = tie(got_a[h], got_b[h], terms[0], base_sum)
            if step == last and h == 0:
                got_a[h], got_b[h], early = tie(got_a[h], got_b[h], early)
            outs = [((half, width_part), BF16)] * (2 * (2 // len(got_a)))
            sends = local_kernel(
                f"send_{step}_{h}",
                functools.partial(send_kernel, sides, owners, h * half),
                outs,
                terms[step],
                terms[owners - step] if sides[1][3] else terms[step],
                late=[got_b[h], got_a[h]],
                flops=SEND_FLOPS[h],
            )
            *sends, got_a[h], got_b[h], x_late, places_here = tie(
                *sends, got_a[h], got_b[h], x, places
            )
            if step > 1 and h == 0:
                low = pick(
                    f"pick_{step - 1}", arrived, places, x_late, per_owner, low, flops=SLOT_FLOPS
                )
            if step == 1:
                (terms[0],) = outer_terms(
                    "term_own", back, places_here, x, [fixed(0)], [F32], per_owner, 1.0
                )
                base_give, cot_here, _ = tie(base_give, cot, sends[0])
                base_sum = base_keep + swap_narrow(base_give, near_bit)
                cots = {0: cot_here, near_bit: cot_near}
                for bit in far_bits:
                    block = swap_narrow(jnp.concatenate(list(cots.values()), axis=0), bit)
                    for i, s in enumerate(list(cots)):
                        cots[s | bit] = block[i * tokens : (i + 1) * tokens]
            if step == last - 1 and h == 1:
                near = [(down_own, fixed(0)), (pieces["a", 1], by_side(1, last))]
                near.append((pieces["b", 1], by_side(last, 1)))
                (early,) = local_kernel(
                    "input_early",
                    functools.partial(input_early_kernel, [o for _, o in near], per_owner),
                    [((tokens, width_part), F32)],
                    *back,
                    places_here,
                    late=[d for d, _ in near],
                    stacked=True,
                )
            for i in range(len(sends) // 2):
                next_b.append(shift(sends[len(sends) // 2 + i], pairs_b))
                next_a.append(shift(sends[i], pairs_a))
        if live_a:
            pieces["a", step] = got_a
        if live_b:
            pieces["b", step] = got_b
        arrived = [
            (pieces[side, step], arriving(step, side == "a"))
            for side in "ab"
            if (side, step) in pieces
        ]
        if 2 * step == owners:
            arrived = [((got_a, got_b, from_a(step)), by_side(step, owners - step))]
        got_a, got_b = next_a, next_b
    low = pick(f"pick_{last}", arrived, places, x, per_owner, low, True)
    *low, got_a[0], got_b[0] = tie(*low, got_a[0], got_b[0])


    def base_product(*held):
        cots.update(zip(cots, held[1:]))
        return local_kernel(
            "base_back",
            functools.partial(base_back_kernel, parts),
            [((tokens, width_part), F32)],
            *[cots[s] for s in range(parts)],
            weight,
            held[0],
            scratch=[pltpu.VMEM((tokens, parts * value_part), BF16)],
        )

    low, _, (got_a[1], got_b[1], base_back), _ = sum_narrow(
        *low,
        1.0,
        core=(early, *cots.values()),
        during=base_product,
        chips=(got_a[1], got_b[1]),
    )
    base_sum, _ = tie(base_sum, low[0])
    sums = {2 * i: base_sum[i * tokens : (i + 1) * tokens] for i in range(parts // 2)}
    for bit in far_bits[:-1]:
        for s in [s for s in sums if s & bit]:
            got = swap_narrow(sums.pop(s).astype(BF16), bit)
            sums[s ^ bit] = sums[s ^ bit] + got.astype(F32)
    base_came = swap_narrow(sums[far_bits[-1]].astype(BF16), far_bits[-1])
    grad_up, *up_terms = outer_terms(
        "up_terms",
        low,
        places,
        cot,
        [fixed(m) for m in range(owners)],
        [F32] + [BF16] * last,
        per_owner,
        ADAPTER_SCALE,
    )
    *up_terms, places_late = tie(*up_terms[::-1], places)
    up_terms = up_terms[::-1]
    got_up = [
        shift(term, [(d, (d + m) % owners) for d in range(owners)])
        for m, term in enumerate(up_terms, 1)
    ]

    projected = local_kernel(
        "projected",
        functools.partial(projected_kernel, [o for _, o in up_all], per_owner),
        [((tokens, value_part), BF16)],
        sums[0],
        base_came,
        *low,
        places_late,
        late=[u for u, _ in up_all],
    )[0]
    slots = [(pieces["a", last], arriving(last, True))]
    for step in range(2, last):
        a, b = pieces.get(("a", step)), pieces.get(("b", owners - step))
        slots.append(((a, b, from_a(step)) if b is not None else a, by_side(step, owners - step)))
    (input_grad,) = local_kernel(
        "input_grad",
        functools.partial(input_grad_kernel, [o for _, o in slots], per_owner),
        [((tokens, width_part), BF16)],
        base_back,
        *back,
        places_late,
        late=[d for d, _ in slots],
        stacked=True,
    )
    (grad_down,) = local_kernel(
        "grad_down",
        grad_down_kernel,
        [((rows, width_part), F32)],
        terms[0],
        late=[got_a, got_b],
    )

    grad_down, input_grad, projected, *got_up = tie(grad_down, input_grad, projected, *got_up)
    for got in got_up:
        grad_up += got.astype(F32)
    return (
        projected,
        input_grad,
        jnp.swapaxes(grad_down.reshape(per_owner, rank, width_part), 1, 2),
        grad_up.reshape(per_owner, rank, value_part),
    )


def solution(mesh):
    in_specs = (
        P(("groups", "wide"), "narrow"),
        P(("groups", "wide"), None),
        P("narrow", None),
        P(("groups", "wide"), "narrow", None),
        P(("groups", "wide"), None, "narrow"),
        P(("groups", "wide"), "narrow"),
    )
    out_specs = (
        P(("groups", "wide"), "narrow"),
        P(("groups", "wide"), "narrow"),
        P(("groups", "wide"), "narrow", None),
        P(("groups", "wide"), None, "narrow"),
    )
    return jax.shard_map(body, mesh=mesh, in_specs=in_specs, out_specs=out_specs, check_vma=False)
```
